32 devices in a mesh: section: 4 (over z), ctx: 4 (over x, core), dp: 2 (over y).
Axes of the slice: x: 2, y: 2, z: 4, core: 2. Of those that a mesh axis runs over, the one named last changes fastest.
Arguments:
- stream: bfloat16 [4, 256, 8192], P('section', 'dp', 'ctx'), may hold values from -6 to 6
- norm_gain: float32 [4, 8192], P('section', 'ctx'), may hold values from 0.5 to 2
- w_router: bfloat16 [4, 8192], P('section', 'ctx'), may hold values from -0.0625 to 0.0625
- w_gate: bfloat16 [4, 8192, 14336], P('section', 'ctx', 'dp'), may hold values from -0.0625 to 0.0625
- w_up: bfloat16 [4, 8192, 14336], P('section', 'ctx', 'dp'), may hold values from -0.0625 to 0.0625
- w_down: bfloat16 [4, 14336, 8192], P('section', 'dp', 'ctx'), may hold values from -0.046875 to 0.046875
- keep_rows: int32 [2, 4, 2, 32], P(None, 'section', 'dp'), may hold values from -1 to 127, as said below
Outputs:
- advanced: bfloat16 [4, 256, 8192], P('section', 'dp', 'ctx')
The draws below stay inside these ranges and needn't reach their ends.
Inputs may be any that keep to these rules, and one draw needn't show every extreme that they name: `keep_rows`: each list holds distinct row indices first, then -1 in its empty slots. Over the 2 lists of one tick and section exactly 32 rows are kept; in each tick and section some list is full and some is empty.
All inputs are finite; a program needn't handle non-finite values.
Results may differ from the reference program's by a relative error of at most 0.005.
Values may be sent and summed in bfloat16 or wider, within the bound.
A program may use at most 192 MiB of HBM per device.

```python
import math
import jax
import jax.numpy as jnp
from jax import lax

D = 8192
FF = 14336
TOK_DEV = 128
KEEP = 16
CAP = 32
TOKENS = 256
N_SECTION = 4
N_DP = 2


def one_list(subkey):
    pair_count = N_DP // 2
    shift_key, order_key, rows_key = jax.random.split(subkey, 3)
    shifts = jax.random.randint(shift_key, (pair_count,), -KEEP, KEEP + 1)
    shifts = shifts.at[0].set(KEEP)
    counts = jnp.concatenate([KEEP + shifts, KEEP - shifts])
    counts = counts[jax.random.permutation(order_key, N_DP)]
    row_keys = jax.random.split(rows_key, N_DP)
    orders = jax.vmap(lambda one_key: jax.random.permutation(one_key, TOK_DEV))(row_keys)
    orders = (orders - orders[:, :1] + TOK_DEV - 1) % TOK_DEV
    slot_ids = jnp.arange(CAP)
    return jnp.where(slot_ids[None, :] < counts[:, None], orders[:, :CAP], -1).astype(jnp.int32)


def draw_keep_rows(key, part):
    all_keys = jax.random.split(key, 2 * N_SECTION)
    return jax.vmap(one_list)(all_keys).reshape(2, N_SECTION, N_DP, CAP)


def levels(rng, dims, cuts, low, top_value):
    loudness, own = 1.0, jax.random.fold_in(rng, 6)
    for position, blocks in cuts:
        steps = jnp.exp(jax.random.uniform(jax.random.fold_in(own, position), (blocks,), jnp.float32, low / len(cuts), top_value / len(cuts)))
        loudness = loudness * jnp.repeat(steps, dims[position] // blocks).reshape([-1 if axis == position else 1 for axis in range(len(dims))])
    return loudness


def bell_draw(stream_key, dims, scale, bound, cuts=(), kind=jnp.bfloat16):
    loudness = levels(stream_key, dims, cuts, -0.22, 0.18) if cuts else 1.0
    entries = jax.random.normal(stream_key, dims, jnp.float32) * scale * loudness
    return jnp.minimum(jnp.maximum(entries, -bound), bound).astype(kind)


def setup_inputs(seed: int = 0) -> dict:
    key_list = jax.random.split(jax.random.key(seed), 8)
    return {
        "stream": bell_draw(key_list[0], (N_SECTION, TOKENS, D), 1.0, 6.0, ((0, 4), (1, 2), (2, 4))),
        "norm_gain": jnp.clip(jnp.exp(math.log(2.0) - 1.3862944 * jax.random.uniform(key_list[1], (N_SECTION, D), jnp.float32) ** levels(key_list[1], (N_SECTION, D), ((0, 4), (1, 4)), -0.2, 0.2)), 0.5, 2.0),
        "w_router": bell_draw(key_list[2], (N_SECTION, D), D ** -0.5, 0.0625, ((0, 4), (1, 4))),
        "w_gate": bell_draw(key_list[3], (N_SECTION, D, FF), D ** -0.5, 0.0625, ((0, 4), (1, 4), (2, 2))),
        "w_up": bell_draw(key_list[4], (N_SECTION, D, FF), D ** -0.5, 0.0625, ((0, 4), (1, 4), (2, 2))),
        "w_down": bell_draw(key_list[5], (N_SECTION, FF, D), FF ** -0.5, 0.046875, ((0, 4), (1, 2), (2, 4))),
        "keep_rows": draw_keep_rows(jax.random.fold_in(key_list[7], 71), 0),
    }


eps = 1e-05

def routed_layer(stream, keep_list, gain_row, router, w_gate, w_up, w_down):
    groups = keep_list.shape[0]
    tok_dev = stream.shape[0] // groups
    is_kept = (keep_list >= 0).reshape(-1)
    global_rows = (keep_list + jnp.arange(groups, dtype=jnp.int32)[:, None] * tok_dev).reshape(-1).astype(jnp.int32)
    picked = stream[jnp.where(is_kept, global_rows, 0)]
    rows_wide = picked.astype(jnp.float32)
    mean_square = lax.optimization_barrier(jnp.mean(rows_wide * rows_wide, axis=1))
    logits = lax.optimization_barrier(jnp.sum(rows_wide * router.astype(jnp.float32), axis=1))
    normed = (rows_wide * lax.rsqrt(mean_square + eps)[:, None] * gain_row[None, :]).astype(jnp.bfloat16)
    gate_proj = jnp.dot(normed, w_gate, preferred_element_type=jnp.float32)
    upward = jnp.dot(normed, w_up, preferred_element_type=jnp.float32)
    hidden = (jax.nn.silu(gate_proj) * upward).astype(jnp.bfloat16)
    update = jnp.dot(hidden, w_down, preferred_element_type=jnp.float32)
    new_rows = (rows_wide + jax.nn.sigmoid(logits)[:, None] * update).astype(jnp.bfloat16)
    target = jnp.where(is_kept, global_rows, stream.shape[0]).astype(jnp.int32)
    return stream.at[target].set(new_rows, mode='drop')

def reference(stream, norm_gain, w_router, w_gate, w_up, w_down, keep_rows):
    firsts = []
    for section_id in range(N_SECTION):
        firsts.append(routed_layer(stream[section_id], keep_rows[0, section_id], norm_gain[section_id], w_router[section_id], w_gate[section_id], w_up[section_id], w_down[section_id]))
    outputs = [firsts[N_SECTION - 1]]
    for section_id in range(1, N_SECTION):
        outputs.append(routed_layer(firsts[section_id - 1], keep_rows[1, section_id], norm_gain[section_id], w_router[section_id], w_gate[section_id], w_up[section_id], w_down[section_id]))
    return jnp.stack(outputs)
```

```python
import functools
import jax
import jax.numpy as jnp
from jax import lax
from jax.experimental import pallas as pl
from jax.experimental.pallas import tpu as pltpu
from jax.sharding import PartitionSpec as P

eps = 1e-05
F32, BF16 = jnp.float32, jnp.bfloat16
MESH = pl.DeviceIdType.MESH


def from_behind(value, axis, steps):
    count = lax.axis_size(axis)
    pairs = [(source, (source + steps) % count) for source in range(count)]
    return lax.ppermute(value, axis, pairs)


def hidden_block(normed, w_gate, w_up, w_down):
    row_piece = lax.all_gather(normed, "dp", axis=0, tiled=True)
    gate_part = jnp.dot(row_piece, w_gate, preferred_element_type=F32)
    up_part = jnp.dot(row_piece, w_up, preferred_element_type=F32)
    partial_value = jnp.stack([gate_part, up_part], axis=1)
    summed = lax.psum(partial_value, "ctx")
    hidden = (jax.nn.silu(summed[:, 0]) * summed[:, 1]).astype(BF16)
    return lax.psum_scatter(
        jnp.dot(hidden, w_down, preferred_element_type=F32).astype(BF16),
        "dp",
        scatter_dimension=0,
        tiled=True,
    ).astype(F32)


def routed_layer(stream, keep_list, gain_row, router, w_gate, w_up, w_down):
    width = stream.shape[1] * lax.axis_size("ctx")
    is_kept = keep_list >= 0
    picked = jnp.take(stream, jnp.maximum(keep_list, 0), axis=0)
    rows_wide = picked.astype(F32)
    squares = jnp.sum(rows_wide * rows_wide, axis=1)
    logits = jnp.sum(rows_wide * router.astype(F32)[None, :], axis=1)
    squares, logits = lax.psum((squares, logits), "ctx")
    scaling = lax.rsqrt(squares / width + eps)
    normed = jnp.where(
        is_kept[:, None], rows_wide * scaling[:, None] * gain_row[None, :], 0.0
    ).astype(BF16)
    update = hidden_block(normed, w_gate, w_up, w_down)
    new_rows = (rows_wide + jax.nn.sigmoid(logits)[:, None] * update).astype(BF16)
    target = jnp.where(is_kept, keep_list, stream.shape[0])
    return stream.at[target].set(new_rows, mode="drop")


def local(stream, norm_gain, w_router, w_gate, w_up, w_down, keep_rows):
    first_pass = routed_layer(
        stream[0], keep_rows[0, 0, 0], norm_gain[0], w_router[0], w_gate[0], w_up[0], w_down[0]
    )
    passed = from_behind(first_pass, "section", 1)
    second_pass = routed_layer(
        passed, keep_rows[1, 0, 0], norm_gain[0], w_router[0], w_gate[0], w_up[0], w_down[0]
    )
    section_place = lax.axis_index("section")
    result = jnp.where(section_place == 0, passed, second_pass)
    return result[None]


UK, UN = 1024, 512
HALF = UN // 2
STAY = 9
RING = 17
LAG = 3


def rc(src, dst, send, recv, where):
    return pltpu.make_async_remote_copy(
        src_ref=src, dst_ref=dst, send_sem=send, recv_sem=recv,
        device_id=where, device_id_type=MESH,
    )


def kernel(dims, stream, gain, router, keeps, wg, wu, wd, out, buf, pstream,
           klist, kprev, xsend, xrecv, xr, xg, stat_send, stat_recv, rs_b, sig_b,
           part, own, p1send, p1recv, p2send, p2recv, hid, usend, urecv, news,
           newr, b1send, b1recv, msend, mrecv,
           wsem, p1s, p1r, p2s, p2r, p3s, p3r, us, ur, ns, nr, sts, strv,
           misc_s, misc_r):
    n_sec, cap, tok, feat, ff, width = dims
    kh = feat // UK
    nj = ff // UN
    nn = feat // UN
    kd = ff // UK
    gu = 2 * kh
    stay = STAY * gu
    per_tick = nj * gu + nn * kd
    loop_units = per_tick - stay
    total = 2 * loop_units

    sec = lax.axis_index("section")
    ctx = lax.axis_index("ctx")
    dp = lax.axis_index("dp")
    core = ctx % 2
    ctx1 = ctx + 1 - 2 * core
    ctx2 = (ctx + 2) % 4
    ctx3 = 3 - ctx
    nxt = (sec + 1) % n_sec
    prv = (sec + n_sec - 1) % n_sec
    to_dp, to_c1, to_c2, to_c3 = {"dp": 1 - dp}, {"ctx": ctx1}, {"ctx": ctx2}, {"ctx": ctx3}
    to_next, to_prev = {"section": nxt}, {"section": prv}

    def load(slot, u):
        j, i = u // gu, u % gu
        rows = pl.ds(pl.multiple_of((i % kh) * UK, UK), UK)
        cols = pl.ds(pl.multiple_of(j * UN, UN), UN)

        @pl.when((u < nj * gu) & (i < kh))
        def _():
            pltpu.make_async_copy(wg.at[0, rows, cols], buf.at[slot], wsem.at[slot]).start()

        @pl.when((u < nj * gu) & (i >= kh))
        def _():
            pltpu.make_async_copy(wu.at[0, rows, cols], buf.at[slot], wsem.at[slot]).start()

        @pl.when(u >= nj * gu)
        def _():
            v = u - nj * gu
            n, k = v // kd, v % kd
            drows = pl.ds(pl.multiple_of(k * UK, UK), UK)
            dcols = pl.ds(pl.multiple_of(n * UN, UN), UN)
            pltpu.make_async_copy(wd.at[0, drows, dcols], buf.at[slot], wsem.at[slot]).start()

    def arrived(slot):
        pltpu.make_async_copy(
            wg.at[0, pl.ds(0, UK), pl.ds(0, UN)], buf.at[slot], wsem.at[slot]
        ).wait()

    def refill(q):
        later = q + RING

        @pl.when(later < total)
        def _():
            load(stay + q % RING, stay + later % loop_units)

    @pl.loop(0, stay + RING)
    def _(u):
        load(u, u)

    barrier = pltpu.get_barrier_semaphore()
    for where in (to_dp, to_c1, to_c2, to_c3, to_next, to_prev):
        pl.semaphore_signal(barrier, inc=1, device_id=where, device_id_type=MESH)

    diag = lax.broadcasted_iota(jnp.int32, (cap, cap), 0) == lax.broadcasted_iota(
        jnp.int32, (cap, cap), 1)
    lane_tok = lax.broadcasted_iota(jnp.int32, (cap, tok), 1).astype(F32)

    def column(row):
        spread = jnp.where(diag, jnp.broadcast_to(row.astype(F32), (cap, cap)), 0.0)
        return jnp.sum(spread, axis=1, keepdims=True)

    row0 = keeps[0]
    row1 = keeps[1]
    pick0 = (column(row0) == lane_tok).astype(BF16)
    klist[...] = jnp.full(klist.shape, -1, jnp.int32)
    klist[0:1, 0:cap] = row0
    for n in range(nn):
        xsend[n] = jnp.dot(
            pick0, stream[0, :, n * UN:(n + 1) * UN], preferred_element_type=F32
        ).astype(BF16)

    pl.semaphore_wait(barrier, 6)

    xcopy = rc(xsend, xrecv, misc_s.at[0], misc_r.at[0], to_dp)
    xcopy.start()
    kcopy = rc(klist, kprev, misc_s.at[1], misc_r.at[1], to_next)
    kcopy.start()
    scopy = rc(stream.at[0], pstream, misc_s.at[2], misc_r.at[2], to_next)
    scopy.start()
    bcopy = rc(b1send, b1recv, misc_s.at[3], misc_r.at[3], to_dp)
    mcopy = rc(msend, mrecv, misc_s.at[4], misc_r.at[4], to_dp)

    lane = lax.broadcasted_iota(jnp.int32, (cap, 128), 1)

    def stat_copy(t, p):
        return rc(stat_send, stat_recv.at[t, p], sts.at[p], strv.at[t, p],
                  (to_c1, to_c2, to_c3)[p])

    def c1copy(t, j):
        return rc(p1send.at[j], p1recv.at[t, j], p1s.at[j], p1r.at[t, j], to_c1)

    def c2copy(t, j):
        return rc(p2send.at[j], p2recv.at[t, j], p2s.at[j], p2r.at[t, j], to_c2)

    def c3copy(t, j):
        return rc(hid.at[t, j, core], hid.at[t, j, core], p3s.at[j], p3r.at[t, j], to_c1)

    def ucopy(t, n):
        return rc(usend.at[n], urecv.at[t, n], us.at[n], ur.at[t, n], to_dp)

    def ncopy(n):
        return rc(news.at[n], newr.at[n], ns.at[n], nr.at[n], to_next)

    for t in (0, 1):
        if t == 0:
            xcopy.wait_recv()
            for n in range(nn):
                xr[n] = xsend[n].astype(F32) + xrecv[n].astype(F32)
        else:
            bcopy.wait_recv()
            mcopy.wait_recv()
            match = (msend[...].astype(F32) + mrecv[...].astype(F32)).astype(BF16)[:, 0:cap]
            for n in range(nn):
                ncopy(n).wait_recv()
                xr[n] = (
                    b1send[n].astype(F32) + b1recv[n].astype(F32)
                    + jnp.dot(match, newr[n], preferred_element_type=F32)
                )
        ss = jnp.zeros((cap, 1), F32)
        lg = jnp.zeros((cap, 1), F32)
        for n in range(nn):
            block = xr[n]
            cols = slice(n * UN, (n + 1) * UN)
            ss += jnp.sum(block * block, axis=1, keepdims=True)
            lg += jnp.sum(block * router[0:1, cols].astype(F32), axis=1, keepdims=True)
            k, off = (n * UN) // UK, (n * UN) % UK
            xg[k, :, off:off + UN] = (block * gain[0:1, cols]).astype(BF16)
        stat_send[...] = jnp.where(lane < 64, ss, lg)
        for p in range(3):
            stat_copy(t, p).start()

        @pl.loop(0, nj + LAG)
        def _(s):
            @pl.when(s < nj)
            def _():
                def unit(i):
                    u = s * gu + i
                    q = t * loop_units + u - stay
                    slot = jnp.where(u < stay, u, stay + (q + RING * 8) % RING)
                    if t == 0:
                        arrived(slot)
                    else:
                        @pl.when(u >= stay)
                        def _():
                            arrived(slot)
                    return slot, u, q

                for which in range(2):
                    total_part = None
                    for k in range(kh):
                        slot, u, q = unit(which * kh + k)
                        term = jnp.dot(xg[k], buf[slot], preferred_element_type=F32)
                        total_part = term if total_part is None else total_part + term
                        refs = (u, q)

                        @pl.when(refs[0] >= stay)
                        def _():
                            refill(refs[1])
                    rows = slice(which * cap, (which + 1) * cap)
                    part[0, rows, :] = total_part[:, :HALF]
                    part[1, rows, :] = total_part[:, HALF:]
                own[s] = part[core]
                p1send[s] = part[1 - core].astype(BF16)
                c1copy(t, s).start()

            @pl.when((s >= 1) & (s < nj + 1))
            def _():
                j = s - 1
                c1copy(t, j).wait_recv()
                both = own[j] + p1recv[t, j].astype(F32)
                own[j] = both
                p2send[j] = both.astype(BF16)
                c2copy(t, j).start()

            @pl.when(s == LAG)
            def _():
                stats = stat_send[...]
                for p in range(3):
                    stat_copy(t, p).wait()
                    stats = stats + stat_recv[t, p]
                rs_b[...] = jnp.broadcast_to(
                    lax.rsqrt(stats[:, 0:1] / width + eps), rs_b.shape)
                sig_b[...] = jnp.broadcast_to(
                    1.0 / (1.0 + jnp.exp(-stats[:, 64:65])), sig_b.shape)

            @pl.when(s >= LAG)
            def _():
                j = s - LAG
                c2copy(t, j).wait_recv()
                both = own[j] + p2recv[t, j].astype(F32)
                scale = rs_b[:, 0:1]
                g = both[0:cap] * scale
                v = both[cap:2 * cap] * scale
                hid[t, j, core] = (g / (1.0 + jnp.exp(-g)) * v).astype(BF16)
                c3copy(t, j).start()

        if t == 0:
            kcopy.wait()
            scopy.wait()
            rowp = kprev[0:1, 0:cap]
            col1 = column(row1)
            same = (col1 == jnp.broadcast_to(rowp.astype(F32), (cap, cap))) & (col1 >= 0.0)
            same = same.astype(F32)
            fresh = jnp.sum(same, axis=1, keepdims=True) == 0.0
            pick1 = jnp.where(fresh, (col1 == lane_tok).astype(F32), 0.0).astype(BF16)
            msend[...] = jnp.zeros(msend.shape, BF16)
            msend[:, 0:cap] = same.astype(BF16)
            for n in range(nn):
                b1send[n] = jnp.dot(
                    pick1, pstream[:, n * UN:(n + 1) * UN], preferred_element_type=F32
                ).astype(BF16)
            bcopy.start()
            mcopy.start()
        else:
            row_tok = lax.broadcasted_iota(jnp.int32, (tok, cap), 0)
            place = (row_tok == jnp.broadcast_to(kprev[0:1, 0:cap], (tok, cap))).astype(F32)
            kept = jnp.sum(place, axis=1, keepdims=True) > 0.0
            place = place.astype(BF16)
            for n in range(nn):
                cols = slice(n * UN, (n + 1) * UN)
                moved = jnp.dot(place, newr[n], preferred_element_type=F32)
                out[0, :, cols] = jnp.where(
                    kept, moved, pstream[:, cols].astype(F32)).astype(BF16)

        @pl.loop(0, nj)
        def _(j):
            c1copy(t, j).wait_send()
            c2copy(t, j).wait_send()
            c3copy(t, j).wait()

        per = UK // UN

        @pl.loop(0, nn + 1)
        def _(n):
            @pl.when(n < nn)
            def _():
                acc = None
                for k in range(kd):
                    u = nj * gu + n * kd + k
                    q = t * loop_units + u - stay
                    slot = stay + q % RING
                    arrived(slot)
                    lhs = jnp.concatenate(
                        [hid[t, per * k + a, b] for a in range(per) for b in range(2)], axis=1)
                    term = jnp.dot(lhs, buf[slot], preferred_element_type=F32)
                    acc = term if acc is None else acc + term
                    refill(q)
                usend[n] = acc.astype(BF16)
                ucopy(t, n).start()

            @pl.when(n >= 1)
            def _():
                m = n - 1
                ucopy(t, m).wait()
                update = usend[m].astype(F32) + urecv[t, m].astype(F32)
                fresh_rows = (xr[m] + sig_b[:, 0:1] * update).astype(BF16)
                if t == 0:
                    news[m] = fresh_rows
                    ncopy(m).start()
                else:
                    mine = jnp.where(sec == 0, -1, row1)
                    spots = (
                        lax.broadcasted_iota(jnp.int32, (tok, cap), 0)
                        == jnp.broadcast_to(mine, (tok, cap))
                    ).astype(F32)
                    here = jnp.sum(spots, axis=1, keepdims=True) > 0.0
                    moved = jnp.dot(spots.astype(BF16), fresh_rows, preferred_element_type=F32)
                    cols = pl.ds(pl.multiple_of(m * UN, UN), UN)
                    out[0, :, cols] = jnp.where(
                        here, moved, out[0, :, cols].astype(F32)).astype(BF16)

    xcopy.wait_send()
    bcopy.wait_send()
    mcopy.wait_send()
    for n in range(nn):
        ncopy(n).wait_send()


def fused(n_sec, width, stream, norm_gain, w_router, w_gate, w_up, w_down, keep_rows):
    _, tok, feat = stream.shape
    ff = w_gate.shape[2]
    cap = keep_rows.shape[-1]
    gu = 2 * (feat // UK)
    nj, nn = ff // UN, feat // UN
    slots = STAY * gu + RING
    vm, dma = pltpu.VMEM, pltpu.SemaphoreType.DMA
    inside = pl.BlockSpec(memory_space=pltpu.VMEM)
    outside = pl.BlockSpec(memory_space=pl.ANY)
    units = ff * feat * 3
    return pl.pallas_call(
        functools.partial(kernel, (n_sec, cap, tok, feat, ff, width)),
        out_shape=jax.ShapeDtypeStruct(stream.shape, stream.dtype),
        in_specs=[inside] * 4 + [outside] * 3,
        out_specs=inside,
        scratch_shapes=[
            vm((slots, UK, UN), BF16),
            vm((tok, feat), BF16),
            vm((8, 128), jnp.int32),
            vm((8, 128), jnp.int32),
            vm((nn, cap, UN), BF16),
            vm((nn, cap, UN), BF16),
            vm((nn, cap, UN), F32),
            vm((feat // UK, cap, UK), BF16),
            vm((cap, 128), F32),
            vm((2, 3, cap, 128), F32),
            vm((cap, 128), F32),
            vm((cap, 128), F32),
            vm((2, 2 * cap, HALF), F32),
            vm((nj, 2 * cap, HALF), F32),
            vm((nj, 2 * cap, HALF), BF16),
            vm((2, nj, 2 * cap, HALF), BF16),
            vm((nj, 2 * cap, HALF), BF16),
            vm((2, nj, 2 * cap, HALF), BF16),
            vm((2, nj, 2, cap, HALF), BF16),
            vm((nn, cap, UN), BF16),
            vm((2, nn, cap, UN), BF16),
            vm((nn, cap, UN), BF16),
            vm((nn, cap, UN), BF16),
            vm((nn, cap, UN), BF16),
            vm((nn, cap, UN), BF16),
            vm((cap, 128), BF16),
            vm((cap, 128), BF16),
            dma((slots,)),
            dma((nj,)), dma((2, nj)), dma((nj,)), dma((2, nj)), dma((nj,)), dma((2, nj)),
            dma((nn,)), dma((2, nn)), dma((nn,)), dma((nn,)),
            dma((3,)), dma((2, 3)), dma((5,)), dma((5,)),
        ],
        compiler_params=pltpu.CompilerParams(
            collective_id=0, has_side_effects=True, vmem_limit_bytes=63 * 2**20),
        cost_estimate=pl.CostEstimate(
            flops=4 * cap * units, bytes_accessed=3 * units, transcendentals=0),
    )(stream, norm_gain, w_router, keep_rows[:, 0], w_gate, w_up, w_down)


def solution(mesh):
    shape = mesh.shape

    def body(stream, norm_gain, w_router, w_gate, w_up, w_down, keep_rows):
        args = (stream, norm_gain, w_router, w_gate, w_up, w_down, keep_rows)
        if shape["dp"] == 2 and shape["ctx"] == 4 and shape["section"] > 2:
            width = stream.shape[2] * shape["ctx"]
            return fused(shape["section"], width, *args)
        return local(*args)

    return jax.shard_map(
        body,
        mesh=mesh,
        in_specs=(
            P("section", "dp", "ctx"),
            P("section", "ctx"),
            P("section", "ctx"),
            P("section", "ctx", "dp"),
            P("section", "ctx", "dp"),
            P("section", "dp", "ctx"),
            P(None, "section", "dp", None),
        ),
        out_specs=P("section", "dp", "ctx"),
        check_vma=False,
    )
```

```python
import functools
import jax
import jax.numpy as jnp
from jax import lax
from jax.experimental import pallas as pl
from jax.experimental.pallas import tpu as pltpu
from jax.sharding import PartitionSpec as P

eps = 1e-05
F32, BF16 = jnp.float32, jnp.bfloat16
MESH = pl.DeviceIdType.MESH


def from_behind(value, axis, steps):
    count = lax.axis_size(axis)
    pairs = [(source, (source + steps) % count) for source in range(count)]
    return lax.ppermute(value, axis, pairs)


def hidden_block(normed, w_gate, w_up, w_down):
    row_piece = lax.all_gather(normed, "dp", axis=0, tiled=True)
    gate_part = jnp.dot(row_piece, w_gate, preferred_element_type=F32)
    up_part = jnp.dot(row_piece, w_up, preferred_element_type=F32)
    partial_value = jnp.stack([gate_part, up_part], axis=1)
    summed = lax.psum(partial_value, "ctx")
    hidden = (jax.nn.silu(summed[:, 0]) * summed[:, 1]).astype(BF16)
    return lax.psum_scatter(
        jnp.dot(hidden, w_down, preferred_element_type=F32).astype(BF16),
        "dp",
        scatter_dimension=0,
        tiled=True,
    ).astype(F32)


def routed_layer(stream, keep_list, gain_row, router, w_gate, w_up, w_down):
    width = stream.shape[1] * lax.axis_size("ctx")
    is_kept = keep_list >= 0
    picked = jnp.take(stream, jnp.maximum(keep_list, 0), axis=0)
    rows_wide = picked.astype(F32)
    squares = jnp.sum(rows_wide * rows_wide, axis=1)
    logits = jnp.sum(rows_wide * router.astype(F32)[None, :], axis=1)
    squares, logits = lax.psum((squares, logits), "ctx")
    scaling = lax.rsqrt(squares / width + eps)
    normed = jnp.where(
        is_kept[:, None], rows_wide * scaling[:, None] * gain_row[None, :], 0.0
    ).astype(BF16)
    update = hidden_block(normed, w_gate, w_up, w_down)
    new_rows = (rows_wide + jax.nn.sigmoid(logits)[:, None] * update).astype(BF16)
    target = jnp.where(is_kept, keep_list, stream.shape[0])
    return stream.at[target].set(new_rows, mode="drop")


def local(stream, norm_gain, w_router, w_gate, w_up, w_down, keep_rows):
    first_pass = routed_layer(
        stream[0], keep_rows[0, 0, 0], norm_gain[0], w_router[0], w_gate[0], w_up[0], w_down[0]
    )
    passed = from_behind(first_pass, "section", 1)
    second_pass = routed_layer(
        passed, keep_rows[1, 0, 0], norm_gain[0], w_router[0], w_gate[0], w_up[0], w_down[0]
    )
    section_place = lax.axis_index("section")
    result = jnp.where(section_place == 0, passed, second_pass)
    return result[None]


UK, UN = 1024, 512
HALF = UN // 2
STAY = 9
RING = 17
LAG = 3


def rc(src, dst, send, recv, where):
    return pltpu.make_async_remote_copy(
        src_ref=src, dst_ref=dst, send_sem=send, recv_sem=recv,
        device_id=where, device_id_type=MESH,
    )


def kernel(dims, stream, gain, router, keeps, wg, wu, wd, out, buf, pstream,
           klist, kprev, xsend, xrecv, xr, xg, stat_send, stat_recv, rs_b, sig_b,
           part, own, p1send, p1recv, p2send, p2recv, hid, usend, urecv, news,
           newr, b1send, b1recv, msend, mrecv,
           wsem, p1s, p1r, p2s, p2r, p3s, p3r, us, ur, ns, nr, sts, strv,
           misc_s, misc_r):
    n_sec, cap, tok, feat, ff, width = dims
    kh = feat // UK
    nj = ff // UN
    nn = feat // UN
    kd = ff // UK
    gu = 2 * kh
    stay = STAY * gu
    per_tick = nj * gu + nn * kd
    loop_units = per_tick - stay
    total = 2 * loop_units

    sec = lax.axis_index("section")
    ctx = lax.axis_index("ctx")
    dp = lax.axis_index("dp")
    core = ctx % 2
    ctx1 = ctx + 1 - 2 * core
    ctx2 = (ctx + 2) % 4
    ctx3 = 3 - ctx
    nxt = (sec + 1) % n_sec
    prv = (sec + n_sec - 1) % n_sec
    to_dp, to_c1, to_c2, to_c3 = {"dp": 1 - dp}, {"ctx": ctx1}, {"ctx": ctx2}, {"ctx": ctx3}
    to_next, to_prev = {"section": nxt}, {"section": prv}

    def load(slot, u):
        j, i = u // gu, u % gu
        rows = pl.ds(pl.multiple_of((i % kh) * UK, UK), UK)
        cols = pl.ds(pl.multiple_of(j * UN, UN), UN)

        @pl.when((u < nj * gu) & (i < kh))
        def _():
            pltpu.make_async_copy(wg.at[0, rows, cols], buf.at[slot], wsem.at[slot]).start()

        @pl.when((u < nj * gu) & (i >= kh))
        def _():
            pltpu.make_async_copy(wu.at[0, rows, cols], buf.at[slot], wsem.at[slot]).start()

        @pl.when(u >= nj * gu)
        def _():
            v = u - nj * gu
            n, k = v // kd, v % kd
            drows = pl.ds(pl.multiple_of(k * UK, UK), UK)
            dcols = pl.ds(pl.multiple_of(n * UN, UN), UN)
            pltpu.make_async_copy(wd.at[0, drows, dcols], buf.at[slot], wsem.at[slot]).start()

    def arrived(slot):
        pltpu.make_async_copy(
            wg.at[0, pl.ds(0, UK), pl.ds(0, UN)], buf.at[slot], wsem.at[slot]
        ).wait()

    def refill(q):
        later = q + RING

        @pl.when(later < total)
        def _():
            load(stay + q % RING, stay + later % loop_units)

    @pl.loop(0, stay + RING)
    def _(u):
        load(u, u)

    barrier = pltpu.get_barrier_semaphore()
    for where in (to_dp, to_c1, to_c2, to_c3, to_next, to_prev):
        pl.semaphore_signal(barrier, inc=1, device_id=where, device_id_type=MESH)

    diag = lax.broadcasted_iota(jnp.int32, (cap, cap), 0) == lax.broadcasted_iota(
        jnp.int32, (cap, cap), 1)
    lane_tok = lax.broadcasted_iota(jnp.int32, (cap, tok), 1).astype(F32)

    def column(row):
        spread = jnp.where(diag, jnp.broadcast_to(row.astype(F32), (cap, cap)), 0.0)
        return jnp.sum(spread, axis=1, keepdims=True)

    row0 = keeps[0]
    row1 = keeps[1]
    pick0 = (column(row0) == lane_tok).astype(BF16)
    klist[...] = jnp.full(klist.shape, -1, jnp.int32)
    klist[0:1, 0:cap] = row0
    for n in range(nn):
        xsend[n] = jnp.dot(
            pick0, stream[0, :, n * UN:(n + 1) * UN], preferred_element_type=F32
        ).astype(BF16)

    pl.semaphore_wait(barrier, 6)

    xcopy = rc(xsend, xrecv, misc_s.at[0], misc_r.at[0], to_dp)
    xcopy.start()
    kcopy = rc(klist, kprev, misc_s.at[1], misc_r.at[1], to_next)
    kcopy.start()
    scopy = rc(stream.at[0], pstream, misc_s.at[2], misc_r.at[2], to_next)
    scopy.start()
    bcopy = rc(b1send, b1recv, misc_s.at[3], misc_r.at[3], to_dp)
    mcopy = rc(msend, mrecv, misc_s.at[4], misc_r.at[4], to_dp)

    lane = lax.broadcasted_iota(jnp.int32, (cap, 128), 1)

    def stat_copy(t, p):
        return rc(stat_send, stat_recv.at[t, p], sts.at[p], strv.at[t, p],
                  (to_c1, to_c2, to_c3)[p])

    def c1copy(t, j):
        return rc(p1send.at[j], p1recv.at[t, j], p1s.at[j], p1r.at[t, j], to_c1)

    def c2copy(t, j):
        return rc(p2send.at[j], p2recv.at[t, j], p2s.at[j], p2r.at[t, j], to_c2)

    def c3copy(t, j):
        return rc(hid.at[t, j, core], hid.at[t, j, core], p3s.at[j], p3r.at[t, j], to_c1)

    def ucopy(t, n):
        return rc(usend.at[n], urecv.at[t, n], us.at[n], ur.at[t, n], to_dp)

    def ncopy(n):
        return rc(news.at[n], newr.at[n], ns.at[n], nr.at[n], to_next)

    for t in (0, 1):
        if t == 0:
            xcopy.wait_recv()
            for n in range(nn):
                xr[n] = xsend[n].astype(F32) + xrecv[n].astype(F32)
        else:
            bcopy.wait_recv()
            mcopy.wait_recv()
            match = (msend[...].astype(F32) + mrecv[...].astype(F32)).astype(BF16)[:, 0:cap]
            for n in range(nn):
                ncopy(n).wait_recv()
                xr[n] = (
                    b1send[n].astype(F32) + b1recv[n].astype(F32)
                    + jnp.dot(match, newr[n], preferred_element_type=F32)
                )
        ss = jnp.zeros((cap, 1), F32)
        lg = jnp.zeros((cap, 1), F32)
        for n in range(nn):
            block = xr[n]
            cols = slice(n * UN, (n + 1) * UN)
            ss += jnp.sum(block * block, axis=1, keepdims=True)
            lg += jnp.sum(block * router[0:1, cols].astype(F32), axis=1, keepdims=True)
            k, off = (n * UN) // UK, (n * UN) % UK
            xg[k, :, off:off + UN] = (block * gain[0:1, cols]).astype(BF16)
        stat_send[...] = jnp.where(lane < 64, ss, lg)
        for p in range(3):
            stat_copy(t, p).start()

        @pl.loop(0, nj + LAG)
        def _(s):
            @pl.when(s < nj)
            def _():
                units = []
                for i in range(gu):
                    u = s * gu + i
                    q = t * loop_units + u - stay
                    units.append((jnp.where(u < stay, u, stay + (q + RING * 8) % RING), q))

                def wait_all():
                    for slot, _ in units:
                        arrived(slot)

                if t == 0:
                    wait_all()
                else:
                    pl.when(s >= STAY)(wait_all)

                for which in range(2):
                    total_part = None
                    for k in range(kh):
                        slot = units[which * kh + k][0]
                        term = jnp.dot(xg[k], buf[slot], preferred_element_type=F32)
                        total_part = term if total_part is None else total_part + term
                    rows = slice(which * cap, (which + 1) * cap)
                    part[0, rows, :] = total_part[:, :HALF]
                    part[1, rows, :] = total_part[:, HALF:]
                own[s] = part[core]
                p1send[s] = part[1 - core].astype(BF16)
                c1copy(t, s).start()

                @pl.when(s >= STAY)
                def _():
                    for _, q in units:
                        refill(q)

            @pl.when((s >= 1) & (s < nj + 1))
            def _():
                j = s - 1
                c1copy(t, j).wait_recv()
                both = own[j] + p1recv[t, j].astype(F32)
                own[j] = both
                p2send[j] = both.astype(BF16)
                c2copy(t, j).start()

            @pl.when(s == LAG)
            def _():
                stats = stat_send[...]
                for p in range(3):
                    stat_copy(t, p).wait()
                    stats = stats + stat_recv[t, p]
                rs_b[...] = jnp.broadcast_to(
                    lax.rsqrt(stats[:, 0:1] / width + eps), rs_b.shape)
                sig_b[...] = jnp.broadcast_to(
                    1.0 / (1.0 + jnp.exp(-stats[:, 64:65])), sig_b.shape)

            @pl.when(s >= LAG)
            def _():
                j = s - LAG
                c2copy(t, j).wait_recv()
                both = own[j] + p2recv[t, j].astype(F32)
                scale = rs_b[:, 0:1]
                g = both[0:cap] * scale
                v = both[cap:2 * cap] * scale
                hid[t, j, core] = (g / (1.0 + jnp.exp(-g)) * v).astype(BF16)
                c3copy(t, j).start()

        if t == 0:
            kcopy.wait()
            scopy.wait()
            rowp = kprev[0:1, 0:cap]
            col1 = column(row1)
            same = (col1 == jnp.broadcast_to(rowp.astype(F32), (cap, cap))) & (col1 >= 0.0)
            same = same.astype(F32)
            fresh = jnp.sum(same, axis=1, keepdims=True) == 0.0
            pick1 = jnp.where(fresh, (col1 == lane_tok).astype(F32), 0.0).astype(BF16)
            msend[...] = jnp.zeros(msend.shape, BF16)
            msend[:, 0:cap] = same.astype(BF16)
            for n in range(nn):
                b1send[n] = jnp.dot(
                    pick1, pstream[:, n * UN:(n + 1) * UN], preferred_element_type=F32
                ).astype(BF16)
            bcopy.start()
            mcopy.start()
        else:
            row_tok = lax.broadcasted_iota(jnp.int32, (tok, cap), 0)
            place = (row_tok == jnp.broadcast_to(kprev[0:1, 0:cap], (tok, cap))).astype(F32)
            kept = jnp.sum(place, axis=1, keepdims=True) > 0.0
            place = place.astype(BF16)
            for n in range(nn):
                cols = slice(n * UN, (n + 1) * UN)
                moved = jnp.dot(place, newr[n], preferred_element_type=F32)
                out[0, :, cols] = jnp.where(
                    kept, moved, pstream[:, cols].astype(F32)).astype(BF16)

        @pl.loop(0, nj)
        def _(j):
            c1copy(t, j).wait_send()
            c2copy(t, j).wait_send()
            c3copy(t, j).wait()

        per = UK // UN

        @pl.loop(0, nn + 1)
        def _(n):
            @pl.when(n < nn)
            def _():
                first = t * loop_units + nj * gu + n * kd - stay
                for k in range(kd):
                    arrived(stay + (first + k) % RING)
                acc = None
                for k in range(kd):
                    lhs = jnp.concatenate(
                        [hid[t, per * k + a, b] for a in range(per) for b in range(2)], axis=1)
                    term = jnp.dot(
                        lhs, buf[stay + (first + k) % RING], preferred_element_type=F32)
                    acc = term if acc is None else acc + term
                usend[n] = acc.astype(BF16)
                ucopy(t, n).start()
                for k in range(kd):
                    refill(first + k)

            @pl.when(n >= 1)
            def _():
                m = n - 1
                ucopy(t, m).wait()
                update = usend[m].astype(F32) + urecv[t, m].astype(F32)
                fresh_rows = (xr[m] + sig_b[:, 0:1] * update).astype(BF16)
                if t == 0:
                    news[m] = fresh_rows
                    ncopy(m).start()
                else:
                    mine = jnp.where(sec == 0, -1, row1)
                    spots = (
                        lax.broadcasted_iota(jnp.int32, (tok, cap), 0)
                        == jnp.broadcast_to(mine, (tok, cap))
                    ).astype(F32)
                    here = jnp.sum(spots, axis=1, keepdims=True) > 0.0
                    moved = jnp.dot(spots.astype(BF16), fresh_rows, preferred_element_type=F32)
                    cols = pl.ds(pl.multiple_of(m * UN, UN), UN)
                    out[0, :, cols] = jnp.where(
                        here, moved, out[0, :, cols].astype(F32)).astype(BF16)

    xcopy.wait_send()
    bcopy.wait_send()
    mcopy.wait_send()
    for n in range(nn):
        ncopy(n).wait_send()


def fused(n_sec, width, stream, norm_gain, w_router, w_gate, w_up, w_down, keep_rows):
    _, tok, feat = stream.shape
    ff = w_gate.shape[2]
    cap = keep_rows.shape[-1]
    gu = 2 * (feat // UK)
    nj, nn = ff // UN, feat // UN
    slots = STAY * gu + RING
    vm, dma = pltpu.VMEM, pltpu.SemaphoreType.DMA
    inside = pl.BlockSpec(memory_space=pltpu.VMEM)
    outside = pl.BlockSpec(memory_space=pl.ANY)
    units = ff * feat * 3
    return pl.pallas_call(
        functools.partial(kernel, (n_sec, cap, tok, feat, ff, width)),
        out_shape=jax.ShapeDtypeStruct(stream.shape, stream.dtype),
        in_specs=[inside] * 4 + [outside] * 3,
        out_specs=inside,
        scratch_shapes=[
            vm((slots, UK, UN), BF16),
            vm((tok, feat), BF16),
            vm((8, 128), jnp.int32),
            vm((8, 128), jnp.int32),
            vm((nn, cap, UN), BF16),
            vm((nn, cap, UN), BF16),
            vm((nn, cap, UN), F32),
            vm((feat // UK, cap, UK), BF16),
            vm((cap, 128), F32),
            vm((2, 3, cap, 128), F32),
            vm((cap, 128), F32),
            vm((cap, 128), F32),
            vm((2, 2 * cap, HALF), F32),
            vm((nj, 2 * cap, HALF), F32),
            vm((nj, 2 * cap, HALF), BF16),
            vm((2, nj, 2 * cap, HALF), BF16),
            vm((nj, 2 * cap, HALF), BF16),
            vm((2, nj, 2 * cap, HALF), BF16),
            vm((2, nj, 2, cap, HALF), BF16),
            vm((nn, cap, UN), BF16),
            vm((2, nn, cap, UN), BF16),
            vm((nn, cap, UN), BF16),
            vm((nn, cap, UN), BF16),
            vm((nn, cap, UN), BF16),
            vm((nn, cap, UN), BF16),
            vm((cap, 128), BF16),
            vm((cap, 128), BF16),
            dma((slots,)),
            dma((nj,)), dma((2, nj)), dma((nj,)), dma((2, nj)), dma((nj,)), dma((2, nj)),
            dma((nn,)), dma((2, nn)), dma((nn,)), dma((nn,)),
            dma((3,)), dma((2, 3)), dma((5,)), dma((5,)),
        ],
        compiler_params=pltpu.CompilerParams(
            collective_id=0, has_side_effects=True, vmem_limit_bytes=63 * 2**20),
        cost_estimate=pl.CostEstimate(
            flops=4 * cap * units, bytes_accessed=3 * units, transcendentals=0),
    )(stream, norm_gain, w_router, keep_rows[:, 0], w_gate, w_up, w_down)


def solution(mesh):
    shape = mesh.shape

    def body(stream, norm_gain, w_router, w_gate, w_up, w_down, keep_rows):
        args = (stream, norm_gain, w_router, w_gate, w_up, w_down, keep_rows)
        if shape["dp"] == 2 and shape["ctx"] == 4 and shape["section"] > 2:
            width = stream.shape[2] * shape["ctx"]
            return fused(shape["section"], width, *args)
        return local(*args)

    return jax.shard_map(
        body,
        mesh=mesh,
        in_specs=(
            P("section", "dp", "ctx"),
            P("section", "ctx"),
            P("section", "ctx"),
            P("section", "ctx", "dp"),
            P("section", "ctx", "dp"),
            P("section", "dp", "ctx"),
            P(None, "section", "dp", None),
        ),
        out_specs=P("section", "dp", "ctx"),
        check_vma=False,
    )
```
